32 devices in a mesh: row: 8 (over z, x), col: 4 (over y, core).
Axes of the slice: x: 2, y: 2, z: 4, core: 2. Of those that a mesh axis runs over, the one named last changes fastest.
Arguments:
- marine_skin_quantities: float32 [5, 256, 512], P(None, 'row', 'col'), may hold values from -6 to 6
- marine_frozen_motion: float32 [2, 8, 16, 1024], P(None, 'row', 'col'), may hold values from -3 to 3
- floe_tensor_components: float32 [3, 8, 16, 1024], P(None, 'row', 'col'), may hold values from -3 to 3
- marine_frozen_weight: float32 [8, 16, 1024], P('row', 'col'), may hold values from 0.5 to 5
- floe_compressive_resistance: float32 [8, 16, 1024], P('row', 'col'), may hold values from 0.2 to 2
- ply_frozen_warmth: float32 [7, 8, 16, 1024], P(None, 'row', 'col'), may hold values from -15 to -2
- filled_places_each_chip: int32 [8, 4], P('row', 'col'), may hold values from 2 to 4, as said below
- frozen_presence_flags: int32 [8, 16], P('row', 'col'), may hold values from 0 to 1, as said below
- frozen_parent_grid_line: int32 [8, 16], P('row', 'col'), may hold values from -1 to 15, as said below
- adjacent_places: int32 [4, 8, 16], P(None, 'row', 'col'), may hold values from -1 to 127, as said below
Outputs:
- ice_velocity_new: float32 [2, 8, 16, 1024], P(None, 'row', 'col')
- ice_stress_new: float32 [3, 8, 16, 1024], P(None, 'row', 'col')
- ice_temperature_new: float32 [7, 8, 16, 1024], P(None, 'row', 'col')
- ocean_forcing: float32 [3, 256, 512], P(None, 'row', 'col')
The draws below stay inside these ranges and needn't reach their ends.
Inputs may be any that keep to these rules, and one draw needn't show every extreme that they name: `filled_places_each_chip`: each device's count lies between 2 and 4; in every row some device has exactly 4. `frozen_presence_flags`: in each row of blocks the ice-covered blocks, in order of column, are dealt to the devices of that row in order, each device as many as its count. `frozen_parent_grid_line`: -1 marks slots beyond a device's count. A device's used slots hold, in order, consecutive ice-covered blocks of its row, all in its own ocean tile or in the tile just before it along col, at most 2 in the tile before; in every row some device holds exactly 2 from the tile before. `adjacent_places`: north is the next row of blocks, east the next block column (columns are periodic). -1 where the neighbor block is not ice-covered, lies beyond the first or last row of blocks, or the slot is unused.
All inputs are finite; a program needn't handle non-finite values.
Results may differ from the reference program's by a relative error of at most 0.0003.
Values sent between devices are 32-bit elements; how exact they have to be, the bound alone decides.
A program may use at most 64 MiB of HBM per device.

```python
import math
import jax
import jax.numpy as jnp
from jax import lax

EDGE = 32
BMAX = 4
FROZEN_PLIES = 7
SUBCYCLES = 4
PATCH_POINTS = 1024
LINE_PLACES = 16
NLONB = 16
NLAT = 256
NLON = 512
N_ROW = 8
N_COL = 4


def ice_layout(key):
    half_slots = BMAX // 2
    full_column = jax.random.randint(jax.random.fold_in(key, 101), (N_ROW,), 1, N_COL)
    counts_drawn = jax.random.randint(jax.random.fold_in(key, 102), (N_ROW, N_COL), half_slots, BMAX + 1)
    columns = jnp.arange(N_COL)[None, :]
    counts_drawn = jnp.where(columns == full_column[:, None] - 1, half_slots, counts_drawn)
    counts_drawn = jnp.where(columns == full_column[:, None], BMAX, counts_drawn).astype(jnp.int32)
    step_key = jax.random.fold_in(key, 103)

    def advance(previous, column):
        upper_limit = jnp.minimum(half_slots, BMAX - counts_drawn[:, column - 1] + previous)
        fresh_draw = jax.random.randint(jax.random.fold_in(step_key, column), (N_ROW,), 0, upper_limit + 1)
        chosen = jnp.where(column == full_column, half_slots, fresh_draw).astype(jnp.int32)
        return (chosen, chosen)
    zero_start = jnp.zeros((N_ROW,), jnp.int32)
    ignored, later_values = lax.scan(advance, zero_start, jnp.arange(1, N_COL))
    carried_in = jnp.concatenate([zero_start[:, None], later_values.T], axis=1)
    carried_out = jnp.concatenate([later_values.T, zero_start[:, None]], axis=1)
    covered_count = counts_drawn + carried_out - carried_in
    scores = jax.random.randint(jax.random.fold_in(key, 104), (N_ROW, N_COL, BMAX), 0, 1 << 20) * BMAX + jnp.arange(BMAX)
    ice_ranks = jnp.argsort(jnp.argsort(scores, axis=-1), axis=-1)
    frozen_presence_flags = (ice_ranks < covered_count[:, :, None]).astype(jnp.int32).reshape(N_ROW, N_COL * BMAX)
    total_blocks = N_COL * BMAX
    places = jnp.arange(total_blocks)[None, :]
    ice_order = jnp.argsort(jnp.where(frozen_presence_flags == 1, places, places + total_blocks), axis=1)
    starts = jnp.cumsum(counts_drawn, axis=1) - counts_drawn
    positions = (starts[:, :, None] + jnp.arange(BMAX)[None, None, :]).reshape(N_ROW, total_blocks)
    slot_alive = (jnp.arange(BMAX)[None, None, :] < counts_drawn[:, :, None]).reshape(N_ROW, total_blocks)
    picked = jnp.take_along_axis(ice_order, jnp.clip(positions, 0, total_blocks - 1), axis=1)
    source = jnp.where(slot_alive, picked, -1).astype(jnp.int32)
    return (counts_drawn, frozen_presence_flags, source)


def draw_filled_places_each_chip(key, part):
    counts_drawn, frozen_presence_flags, source = ice_layout(key)
    return counts_drawn


def draw_frozen_presence_flags(key, part):
    counts_drawn, frozen_presence_flags, source = ice_layout(key)
    return frozen_presence_flags


def draw_frozen_parent_grid_line(key, part):
    counts_drawn, frozen_presence_flags, source = ice_layout(key)
    return source


def draw_adjacent_places(key, part):
    counts_drawn, frozen_presence_flags, source = ice_layout(key)
    slot_width = N_COL * BMAX
    total_blocks = N_COL * BMAX
    row_grid = jnp.repeat(jnp.arange(N_ROW)[:, None], slot_width, axis=1)
    global_slot = (row_grid * slot_width + jnp.arange(slot_width)[None, :]).astype(jnp.int32)
    owner_slot = jnp.full((N_ROW, total_blocks), -1, jnp.int32).at[row_grid, jnp.where(source >= 0, source, total_blocks)].set(global_slot, mode='drop')
    edge_rows = jnp.full((1, total_blocks), -1, jnp.int32)
    padded_owner = jnp.concatenate([edge_rows, owner_slot, edge_rows], axis=0)
    block_place = jnp.clip(source, 0, total_blocks - 1)
    north_link = padded_owner[row_grid + 2, block_place]
    south_link = padded_owner[row_grid, block_place]
    east_link = owner_slot[row_grid, (block_place + 1) % total_blocks]
    west_link = owner_slot[row_grid, (block_place - 1) % total_blocks]
    result = jnp.stack([north_link, south_link, east_link, west_link])
    return jnp.where(source[None, :, :] >= 0, result, -1).astype(jnp.int32)


def level_of(rng, dims, pieces, low, top_value):
    factor_of, own = 1.0, jax.random.fold_in(rng, 6)
    for axis_at, shards_of in pieces:
        steps = jnp.exp(jax.random.uniform(jax.random.fold_in(own, axis_at), (shards_of,), jnp.float32, low / len(pieces), top_value / len(pieces)))
        factor_of = factor_of * jnp.repeat(steps, dims[axis_at] // shards_of).reshape([-1 if axis == axis_at else 1 for axis in range(len(dims))])
    return factor_of


def noise(rng, shape, scale, limit, split=(), held_as=jnp.bfloat16):
    entries = scale * jax.random.normal(rng, shape, jnp.float32)
    if split:
        entries = entries * level_of(rng, shape, split, -0.22, 0.18)
    return jnp.clip(entries, -limit, limit).astype(held_as)


def setup_inputs(seed: int = 0) -> dict:
    seeds = jax.random.split(jax.random.key(seed), 11)
    return {
        "marine_skin_quantities": noise(seeds[0], (5, NLAT, NLON), 1.0, 6.0, ((1, 8), (2, 4)), jnp.float32),
        "marine_frozen_motion": noise(seeds[1], (2, N_ROW, LINE_PLACES, PATCH_POINTS), 0.5, 3.0, ((1, 8), (2, 4)), jnp.float32),
        "floe_tensor_components": noise(seeds[2], (3, N_ROW, LINE_PLACES, PATCH_POINTS), 0.5, 3.0, ((1, 8), (2, 4)), jnp.float32),
        "marine_frozen_weight": jnp.clip(jnp.exp(math.log(5.0) - 2.3025851 * jax.random.uniform(seeds[3], (N_ROW, LINE_PLACES, PATCH_POINTS), jnp.float32) ** level_of(seeds[3], (N_ROW, LINE_PLACES, PATCH_POINTS), ((0, 8), (1, 4)), -0.2, 0.2)), 0.5, 5.0),
        "floe_compressive_resistance": jnp.clip(jnp.exp(math.log(2.0) - 2.3025851 * jax.random.uniform(seeds[4], (N_ROW, LINE_PLACES, PATCH_POINTS), jnp.float32) ** level_of(seeds[4], (N_ROW, LINE_PLACES, PATCH_POINTS), ((0, 8), (1, 4)), -0.2, 0.2)), 0.2, 2.0),
        "ply_frozen_warmth": jnp.clip(-15.0 + 13.0 * jax.random.uniform(seeds[5], (FROZEN_PLIES, N_ROW, LINE_PLACES, PATCH_POINTS), jnp.float32) ** level_of(seeds[5], (FROZEN_PLIES, N_ROW, LINE_PLACES, PATCH_POINTS), ((1, 8), (2, 4)), -0.2, 0.2), -15.0, -2.0),
        "filled_places_each_chip": draw_filled_places_each_chip(jax.random.fold_in(seeds[10], 71), 0),
        "frozen_presence_flags": draw_frozen_presence_flags(jax.random.fold_in(seeds[10], 71), 0),
        "frozen_parent_grid_line": draw_frozen_parent_grid_line(jax.random.fold_in(seeds[10], 71), 0),
        "adjacent_places": draw_adjacent_places(jax.random.fold_in(seeds[10], 71), 0),
    }


RELAX_RATE = 0.8
STEP_WEIGHT = 0.5
AIR_DRAG = 0.3
WATER_DRAG = 0.6
TOPMOST_WARMTH = -12.0
FREEZING = -1.8
DIFFUSION = 0.6
THERMAL_KAPPA = 0.1
OPEN_HEAT = 0.4
OPEN_WIND = 0.5

def neighbor_values(field_values, halo_north, halo_south, halo_east, halo_west):
    boundary = halo_north.shape[-1]
    places = jnp.arange(field_values.shape[-1])
    grid_row = places // boundary
    grid_col = places % boundary
    repeats = (1,) * (field_values.ndim - 1) + (boundary,)
    upper_cells = jnp.where(grid_row == boundary - 1, jnp.tile(halo_north, repeats), jnp.roll(field_values, -boundary, axis=-1))
    lower_cells = jnp.where(grid_row == 0, jnp.tile(halo_south, repeats), jnp.roll(field_values, boundary, axis=-1))
    right_cells = jnp.where(grid_col == boundary - 1, jnp.repeat(halo_east, boundary, axis=-1), jnp.roll(field_values, -1, axis=-1))
    left_cells = jnp.where(grid_col == 0, jnp.repeat(halo_west, boundary, axis=-1), jnp.roll(field_values, 1, axis=-1))
    return (upper_cells, lower_cells, right_cells, left_cells)

def stress_update(floe_motion_speed, stress, strength, halo_set):
    upper_cells, lower_cells, right_cells, left_cells = neighbor_values(floe_motion_speed, halo_set[0], halo_set[1], halo_set[2], halo_set[3])
    stretch_east = 0.5 * (right_cells[0] - left_cells[0])
    shear_east = 0.5 * (right_cells[1] - left_cells[1])
    shear_north = 0.5 * (upper_cells[0] - lower_cells[0])
    stretch_north = 0.5 * (upper_cells[1] - lower_cells[1])
    shearing = 0.5 * (shear_north + shear_east)
    divergence = stretch_east + stretch_north
    tension = stretch_east - stretch_north
    deformation = jnp.sqrt(divergence * divergence + 0.25 * (tension * tension + 4.0 * shearing * shearing) + 0.25)
    viscosity = strength / (2.0 * deformation)
    common = 0.75 * viscosity * divergence - 0.25 * strength
    target = jnp.stack([0.5 * viscosity * stretch_east + common, 0.5 * viscosity * stretch_north + common, 0.5 * viscosity * shearing])
    return (stress + RELAX_RATE * target) / (1.0 + RELAX_RATE)

def velocity_update(floe_motion_speed, stress, weight_density_sheet, skin_quantities, halo_set):
    upper_cells, lower_cells, right_cells, left_cells = neighbor_values(stress, halo_set[0], halo_set[1], halo_set[2], halo_set[3])
    force_east = 0.5 * (right_cells[0] - left_cells[0]) + 0.5 * (upper_cells[2] - lower_cells[2])
    force_north = 0.5 * (right_cells[2] - left_cells[2]) + 0.5 * (upper_cells[1] - lower_cells[1])
    pushing = jnp.stack([force_east, force_north]) + AIR_DRAG * skin_quantities[3:5] + WATER_DRAG * skin_quantities[1:3]
    return (weight_density_sheet * floe_motion_speed + STEP_WEIGHT * pushing) / (weight_density_sheet + STEP_WEIGHT * WATER_DRAG)

def thermal_diffusive_update(ply_warmth_state, weight_density_sheet, skin_quantities):
    floe_depth_extent = weight_density_sheet / 0.9
    marine_exchange_step = DIFFUSION / (floe_depth_extent * floe_depth_extent)
    diagonal = 1.0 + 2.0 * marine_exchange_step
    ply_sequence = ply_warmth_state.shape[0]
    ratios = []
    partial_values = []
    for depthwise_ply_number in range(ply_sequence):
        warming_supply_rate = ply_warmth_state[depthwise_ply_number]
        if depthwise_ply_number == 0:
            warming_supply_rate = warming_supply_rate + marine_exchange_step * TOPMOST_WARMTH
        if depthwise_ply_number == ply_sequence - 1:
            warming_supply_rate = warming_supply_rate + marine_exchange_step * skin_quantities[0]
        if depthwise_ply_number == 0:
            pivot_value = diagonal
            carried = warming_supply_rate / pivot_value
        else:
            pivot_value = diagonal - marine_exchange_step * ratios[-1]
            carried = (warming_supply_rate + marine_exchange_step * partial_values[-1]) / pivot_value
        ratios.append(marine_exchange_step / pivot_value)
        partial_values.append(carried)
    solved = [partial_values[-1]]
    for depthwise_ply_number in range(ply_sequence - 2, -1, -1):
        solved.insert(0, partial_values[depthwise_ply_number] + ratios[depthwise_ply_number] * solved[0])
    return jnp.stack(solved)

def marine_frozen_exchanges(ply_warmth_state, floe_motion_speed, weight_density_sheet, skin_quantities):
    floe_depth_extent = weight_density_sheet / 0.9
    thermal_transfer_amount = THERMAL_KAPPA * (ply_warmth_state[-1] - skin_quantities[0]) / floe_depth_extent
    return jnp.concatenate([thermal_transfer_amount[None], WATER_DRAG * (floe_motion_speed - skin_quantities[1:3])], axis=0)

def open_water(skin_quantities):
    thermal_transfer_amount = -OPEN_HEAT * (skin_quantities[0] - FREEZING)
    return jnp.concatenate([thermal_transfer_amount[None], OPEN_WIND * skin_quantities[3:5]], axis=0)

def reference(marine_skin_quantities, marine_frozen_motion, floe_tensor_components, marine_frozen_weight, floe_compressive_resistance, ply_frozen_warmth, filled_places_each_chip, frozen_presence_flags, frozen_parent_grid_line, adjacent_places):
    place_overall_sum = N_ROW * LINE_PLACES
    floe_motion_speed = marine_frozen_motion.reshape(2, place_overall_sum, PATCH_POINTS)
    stress = floe_tensor_components.reshape(3, place_overall_sum, PATCH_POINTS)
    weight_density_sheet = marine_frozen_weight.reshape(place_overall_sum, PATCH_POINTS)
    strength = floe_compressive_resistance.reshape(place_overall_sum, PATCH_POINTS)
    ply_warmth_state = ply_frozen_warmth.reshape(FROZEN_PLIES, place_overall_sum, PATCH_POINTS)
    slot_place = jnp.arange(LINE_PLACES, dtype=jnp.int32) % BMAX
    slot_alive = (slot_place[None, :] < jnp.repeat(filled_places_each_chip, BMAX, axis=1)).reshape(place_overall_sum)
    source = frozen_parent_grid_line.reshape(place_overall_sum).astype(jnp.int32)
    row_of = jnp.repeat(jnp.arange(N_ROW, dtype=jnp.int32), LINE_PLACES)
    blocks = marine_skin_quantities.reshape(5, N_ROW, EDGE, NLONB, EDGE).transpose(0, 1, 3, 2, 4).reshape(5, N_ROW, NLONB, PATCH_POINTS)
    skin_quantities = blocks[:, row_of, jnp.clip(source, 0, NLONB - 1)]
    link_ids = adjacent_places.reshape(4, place_overall_sum).astype(jnp.int32)

    def gather_halos(field_values):
        square = field_values.reshape(field_values.shape[0], place_overall_sum, EDGE, EDGE)
        facing = (square[:, :, 0, :], square[:, :, EDGE - 1, :], square[:, :, :, 0], square[:, :, :, EDGE - 1])
        result = []
        for direction in range(4):
            target = link_ids[direction]
            fetched = jnp.take(facing[direction], jnp.clip(target, 0, place_overall_sum - 1), axis=1)
            result.append(jnp.where((target >= 0)[None, :, None], fetched, jnp.zeros_like(fetched)))
        return tuple(result)
    for step_index in range(SUBCYCLES):
        stress = stress_update(floe_motion_speed, stress, strength, gather_halos(floe_motion_speed))
        floe_motion_speed = velocity_update(floe_motion_speed, stress, weight_density_sheet, skin_quantities, gather_halos(stress))
    ply_warmth_state = thermal_diffusive_update(ply_warmth_state, weight_density_sheet, skin_quantities)
    skin_exchanges = marine_frozen_exchanges(ply_warmth_state, floe_motion_speed, weight_density_sheet, skin_quantities)
    keep_flags = slot_alive[None, :, None]
    motion_result = jnp.where(keep_flags, floe_motion_speed, jnp.zeros_like(floe_motion_speed)).reshape(2, N_ROW, LINE_PLACES, PATCH_POINTS)
    tensor_result = jnp.where(keep_flags, stress, jnp.zeros_like(stress)).reshape(3, N_ROW, LINE_PLACES, PATCH_POINTS)
    warmth_result = jnp.where(keep_flags, ply_warmth_state, jnp.zeros_like(ply_warmth_state)).reshape(FROZEN_PLIES, N_ROW, LINE_PLACES, PATCH_POINTS)
    owner_slot = jnp.full((N_ROW, NLONB), -1, dtype=jnp.int32).at[row_of, jnp.where(source >= 0, source, NLONB)].set(jnp.arange(place_overall_sum, dtype=jnp.int32), mode='drop')
    from_ice = jnp.take(skin_exchanges, jnp.clip(owner_slot.reshape(-1), 0, place_overall_sum - 1), axis=1)
    from_open = open_water(blocks.reshape(5, N_ROW * NLONB, PATCH_POINTS))
    covered = (frozen_presence_flags.reshape(-1) == 1)[None, :, None]
    applied_driving_load = jnp.where(covered, from_ice, from_open)
    applied_driving_load = applied_driving_load.reshape(3, N_ROW, NLONB, EDGE, EDGE).transpose(0, 1, 3, 2, 4).reshape(3, NLAT, NLON)
    return (motion_result, tensor_result, warmth_result, applied_driving_load)
```

```python
import jax
import jax.numpy as jnp
from jax import lax
from jax.experimental import pallas as pl
from jax.experimental.pallas import tpu as pltpu
from jax.sharding import PartitionSpec as P

SUBCYCLES = 4
RELAX_RATE = 0.8
STEP_WEIGHT = 0.5
AIR_DRAG = 0.3
WATER_DRAG = 0.6
TOPMOST_WARMTH = -12.0
FREEZING = -1.8
DIFFUSION = 0.6
THERMAL_KAPPA = 0.1
OPEN_HEAT = 0.4
OPEN_WIND = 0.5

EDGE = 32
TILE = 4
MESH = pl.DeviceIdType.MESH


def lanes():
    return lax.broadcasted_iota(jnp.int32, (8, 128), 1)


def swap_groups(a, b, width, low):
    return (
        jnp.where(low, a, pltpu.roll(b, width, 1)),
        jnp.where(low, pltpu.roll(a, 128 - width, 1), b),
    )


def transpose4(parts):
    lane = lanes()
    low64 = lane < 64
    low32 = (lane % 64) < 32
    a, b, c, d = parts
    a, c = swap_groups(a, c, 64, low64)
    b, d = swap_groups(b, d, 64, low64)
    a, b = swap_groups(a, b, 32, low32)
    c, d = swap_groups(c, d, 32, low32)
    return [a, b, c, d]


def pick(parts, index):
    value = parts[0]
    for i in range(1, len(parts)):
        value = jnp.where(index == i, parts[i], value)
    return value


def solve_layers(warm_ref, out_ref, weight, surface, alive):
    layers = warm_ref.shape[0]
    thickness = weight * (1.0 / 0.9)
    inverse = 1.0 / thickness
    c = DIFFUSION * inverse * inverse
    diagonal = 1.0 + 2.0 * c
    ratios, partial = [], []
    for l in range(layers):
        supply = warm_ref[l, 0]
        if l == 0:
            supply = supply + c * TOPMOST_WARMTH
        if l == layers - 1:
            supply = supply + c * surface
        if l == 0:
            pivot = diagonal
        else:
            pivot = diagonal - c * ratios[-1]
            supply = supply + c * partial[-1]
        flip = 1.0 / pivot
        partial.append(supply * flip)
        ratios.append(c * flip)
    value = partial[-1]
    flux = THERMAL_KAPPA * (value - surface) * inverse
    out_ref[layers - 1, 0] = jnp.where(alive, value, 0.0)
    for l in range(layers - 2, -1, -1):
        value = partial[l] + ratios[l] * value
        out_ref[l, 0] = jnp.where(alive, value, 0.0)
    return flux


def kernel(
    rows,
    cols,
    skin, motion, tensor, weight, strength, warm, filled, flags, source,
    motion_out, tensor_out, warm_out, ocean_out,
    B, TS, TSS, HF, F, K, KS, G, D, DS, send, recv,
):
    me_r = lax.axis_index("row")
    me_c = lax.axis_index("col")
    east = (me_r, lax.rem(me_c + 1, cols))
    west = (me_r, lax.rem(me_c + cols - 1, cols))
    north = (me_r + 1, me_c)
    south = (me_r - 1, me_c)
    has_north = me_r < rows - 1
    has_south = me_r > 0

    F[:, :, 8:16, :] = jnp.zeros((9, 4, 8, 128), jnp.float32)
    K[:, :, 8:16, :] = jnp.zeros((2, 4, 8, 128), jnp.float32)

    barrier = pltpu.get_barrier_semaphore()
    pl.semaphore_signal(barrier, inc=1, device_id=east, device_id_type=MESH)
    pl.semaphore_signal(barrier, inc=1, device_id=west, device_id_type=MESH)

    @pl.when(has_north)
    def _():
        pl.semaphore_signal(barrier, inc=1, device_id=north, device_id_type=MESH)

    @pl.when(has_south)
    def _():
        pl.semaphore_signal(barrier, inc=1, device_id=south, device_id_type=MESH)

    first = me_c * TILE
    block_index, block_covered = [], []
    out_rank = jnp.int32(0)
    out_first = jnp.int32(0)
    out_second = jnp.int32(0)
    for b in range(TILE):
        own = jnp.int32(-1)
        for j in range(TILE):
            own = jnp.where(source[0, j] == first + b, j, own)
        covered = flags[0, b] == 1
        moved = jnp.logical_and(covered, own < 0)
        block_index.append(jnp.where(own >= 0, own, TILE + jnp.minimum(out_rank, 1)))
        block_covered.append(covered)
        out_first = jnp.where(jnp.logical_and(moved, out_rank == 0), b, out_first)
        out_second = jnp.where(jnp.logical_and(moved, out_rank == 1), b, out_second)
        out_rank = out_rank + jnp.where(moved, 1, 0)
    slot_index = [
        jnp.where(source[0, j] >= first, jnp.minimum(source[0, j] - first, TILE - 1), TILE + min(j, 1))
        for j in range(TILE)
    ]

    for f in range(2):
        B[0:4, f] = motion[f, 0].reshape(4, 8, 128)
    for f in range(3):
        B[0:4, 2 + f] = tensor[f, 0].reshape(4, 8, 128)
    B[0:4, 5] = weight[0].reshape(4, 8, 128)
    B[0:4, 6] = strength[0].reshape(4, 8, 128)

    surface = transpose4([skin[0, pl.ds(q, 8, stride=4), :] for q in range(4)])
    for b in range(4):
        TS[b] = surface[b]
    TSS[0] = pick(surface, out_first)
    TSS[1] = pick(surface, out_second)

    peers = 2 + jnp.minimum(me_r, 1) + jnp.minimum(rows - 1 - me_r, 1)
    pl.semaphore_wait(barrier, peers)

    def remote(k, src, dst, device):
        return pltpu.make_async_remote_copy(
            src_ref=src, dst_ref=dst, send_sem=send.at[k], recv_sem=recv.at[k],
            device_id=device, device_id_type=MESH,
        )

    slots_west = remote(0, B.at[0:2], B.at[4:6], west)
    slots_west.start()
    temps_east = remote(1, TSS, TS.at[4:6], east)
    temps_east.start()

    for q in range(4):
        at = pl.ds(q, 8, stride=4)
        F[7, q, 0:8] = AIR_DRAG * skin[3, at, :] + WATER_DRAG * skin[1, at, :]
        F[8, q, 0:8] = AIR_DRAG * skin[4, at, :] + WATER_DRAG * skin[2, at, :]

    slots_west.wait_recv()
    group = lanes() // 8
    pack_e = [jnp.zeros((8, 128), jnp.float32)] * 4
    pack_w = [jnp.zeros((8, 128), jnp.float32)] * 4
    for p in range(9):
        if p < 7:
            held = [
                jnp.where(block_covered[b], B[block_index[b], p], 0.0) for b in range(4)
            ]
            held = transpose4(held)
        for q in range(4):
            if p < 7:
                F[p, q, 0:8] = held[q]
                value = held[q]
            else:
                value = F[p, q, 0:8]
            turned = pltpu.roll(value, 8 * p, 1) if p else value
            pack_e[q] = jnp.where(group == p, turned, pack_e[q])
            pack_w[q] = jnp.where(group == (p + 15) % 16, turned, pack_w[q])
    for q in range(4):
        KS[0, q] = pack_e[q]
        KS[1, q] = pack_w[q]

    strip_west = remote(2, KS.at[0], K.at[0, :, 0:8, :], west)
    strip_east = remote(3, KS.at[1], K.at[1, :, 0:8, :], east)
    strip_west.start()
    strip_east.start()
    rows_north = remote(4, F.at[:, :, 6:8, :], F.at[:, :, 14:16, :], north)
    rows_south = remote(5, F.at[:, :, 0:2, :], F.at[:, :, 8:10, :], south)
    corner_north = remote(6, K.at[:, :, 6:8, :], K.at[:, :, 14:16, :], north)
    corner_south = remote(7, K.at[:, :, 0:2, :], K.at[:, :, 8:10, :], south)

    @pl.when(has_north)
    def _():
        rows_north.start()

    @pl.when(has_south)
    def _():
        rows_south.start()

    temps_east.wait_recv()
    slot_row = lax.broadcasted_iota(jnp.int32, (4, 1024), 0)
    alive = slot_row < filled[0, 0]
    slot_surface = jnp.stack([TS[slot_index[j]] for j in range(4)]).reshape(4, 1024)
    flux = solve_layers(warm, warm_out, weight[0], slot_surface, alive)
    HF[0:4] = flux.reshape(4, 8, 128)
    heat_west = remote(8, HF.at[0:2], HF.at[4:6], west)
    heat_west.start()

    strip_west.wait_recv()
    strip_east.wait_recv()

    @pl.when(has_north)
    def _():
        corner_north.start()

    @pl.when(has_south)
    def _():
        corner_south.start()

    @pl.when(has_south)
    def _():
        rows_north.wait_recv()

    @pl.when(has_north)
    def _():
        rows_south.wait_recv()

    @pl.when(has_south)
    def _():
        corner_north.wait_recv()

    @pl.when(has_north)
    def _():
        corner_south.wait_recv()

    wide = lax.broadcasted_iota(jnp.int32, (16, 128), 1) // 8
    for q in range(4):
        from_e = K[0, q]
        from_w = K[1, q]
        planes = []
        for p in range(9):
            side = jnp.where(wide == p, from_e, jnp.where(wide == (p + 15) % 16, from_w, 0.0))
            if p:
                side = pltpu.roll(side, 128 - 8 * p, 1)
            planes.append(jnp.concatenate([F[p, q], side], axis=1))
        for p in range(5):
            G[p, q] = planes[p]
        mass = planes[5]
        icy = mass > 0.0
        flip = jnp.where(icy, 1.0 / (mass + STEP_WEIGHT * WATER_DRAG), 0.0)
        G[5, q] = mass * flip
        G[6, q] = (0.5 * STEP_WEIGHT) * flip
        G[7, q] = planes[6]
        G[8, q] = STEP_WEIGHT * flip * planes[7]
        G[9, q] = STEP_WEIGHT * flip * planes[8]

    def across_x(x):
        return pltpu.roll(x, 255, 1) - pltpu.roll(x, 1, 1)

    def across_y(p, q):
        upper = G[p, q + 1] if q < 3 else pltpu.roll(G[p, 0], 15, 0)
        lower = G[p, q - 1] if q > 0 else pltpu.roll(G[p, 3], 1, 0)
        return upper - lower

    keep = 1.0 / (1.0 + RELAX_RATE)
    mix = RELAX_RATE / (1.0 + RELAX_RATE)

    def subcycle(step, carry):
        for q in range(4):
            ux = across_x(G[0, q])
            vx = across_x(G[1, q])
            uy = across_y(0, q)
            vy = across_y(1, q)
            power = G[7, q]
            divergence = 0.5 * (ux + vy)
            tension = 0.5 * (ux - vy)
            shearing = 0.25 * (uy + vx)
            square = (
                divergence * divergence
                + 0.25 * (tension * tension + 4.0 * shearing * shearing)
                + 0.25
            )
            viscosity = (0.5 * mix) * power * lax.rsqrt(square)
            common = 0.75 * viscosity * divergence - (0.25 * mix) * power
            half = 0.25 * viscosity
            G[2, q] = keep * G[2, q] + half * ux + common
            G[3, q] = keep * G[3, q] + half * vy + common
            G[4, q] = keep * G[4, q] + 0.5 * viscosity * shearing
        for q in range(4):
            force_e = across_x(G[2, q]) + across_y(4, q)
            force_n = across_x(G[4, q]) + across_y(3, q)
            share = G[6, q]
            stay = G[5, q]
            G[0, q] = stay * G[0, q] + share * force_e + G[8, q]
            G[1, q] = stay * G[1, q] + share * force_n + G[9, q]
        return carry

    lax.fori_loop(0, SUBCYCLES, subcycle, 0)

    for p in range(5):
        blocks = transpose4([G[p, q, 0:8, 0:128] for q in range(4)])
        for b in range(4):
            D[b, p] = blocks[b]
        DS[0, p] = pick(blocks, out_first)
        DS[1, p] = pick(blocks, out_second)
    back_east = remote(9, DS, D.at[4:6], east)
    back_east.start()

    heat_west.wait_recv()
    lane_block = lanes() // EDGE
    ice = jnp.zeros((8, 128), jnp.int32)
    for b in range(4):
        ice = jnp.where(lane_block == b, jnp.where(block_covered[b], 1, 0), ice)
    ice = ice == 1
    heat = transpose4([HF[block_index[b]] for b in range(4)])
    for q in range(4):
        at = pl.ds(q, 8, stride=4)
        ocean_out[0, at, :] = jnp.where(ice, heat[q], -OPEN_HEAT * (skin[0, at, :] - FREEZING))
        for f in range(2):
            ocean_out[1 + f, at, :] = jnp.where(
                ice,
                WATER_DRAG * (G[f, q, 0:8, 0:128] - skin[1 + f, at, :]),
                OPEN_WIND * skin[3 + f, at, :],
            )

    back_east.wait_recv()
    for p in range(5):
        value = jnp.stack([D[slot_index[j], p] for j in range(4)]).reshape(4, 1024)
        value = jnp.where(alive, value, 0.0)
        if p < 2:
            motion_out[p, 0] = value
        else:
            tensor_out[p - 2, 0] = value

    for copy in (slots_west, temps_east, strip_west, strip_east, heat_west, back_east):
        copy.wait_send()

    @pl.when(has_north)
    def _():
        rows_north.wait_send()
        corner_north.wait_send()

    @pl.when(has_south)
    def _():
        rows_south.wait_send()
        corner_south.wait_send()


def solution(mesh):
    rows, cols = mesh.shape["row"], mesh.shape["col"]

    def local(skin, motion, tensor, weight, strength, warm, filled, flags, source, adjacent):
        vmem = pl.BlockSpec(memory_space=pltpu.VMEM)
        smem = pl.BlockSpec(memory_space=pltpu.SMEM)
        f32 = jnp.float32

        def body(*refs):
            kernel(rows, cols, *refs)

        return pl.pallas_call(
            body,
            out_shape=tuple(
                jax.ShapeDtypeStruct(s, f32)
                for s in (motion.shape, tensor.shape, warm.shape, (3,) + skin.shape[1:])
            ),
            in_specs=[vmem] * 6 + [smem] * 3,
            out_specs=(vmem,) * 4,
            scratch_shapes=[
                pltpu.VMEM((6, 7, 8, 128), f32),
                pltpu.VMEM((6, 8, 128), f32),
                pltpu.VMEM((2, 8, 128), f32),
                pltpu.VMEM((6, 8, 128), f32),
                pltpu.VMEM((9, 4, 16, 128), f32),
                pltpu.VMEM((2, 4, 16, 128), f32),
                pltpu.VMEM((2, 4, 8, 128), f32),
                pltpu.VMEM((10, 4, 16, 256), f32),
                pltpu.VMEM((6, 5, 8, 128), f32),
                pltpu.VMEM((2, 5, 8, 128), f32),
                pltpu.SemaphoreType.DMA((10,)),
                pltpu.SemaphoreType.DMA((10,)),
            ],
            compiler_params=pltpu.CompilerParams(
                collective_id=0, has_side_effects=True, vmem_limit_bytes=16 * 1024 * 1024
            ),
        )(skin, motion, tensor, weight, strength, warm, filled, flags, source)

    in_specs = (
        P(None, "row", "col"),
        P(None, "row", "col", None),
        P(None, "row", "col", None),
        P("row", "col", None),
        P("row", "col", None),
        P(None, "row", "col"),
        P("row", "col"),
        P("row", "col"),
        P("row", "col"),
        P(None, "row", "col"),
    )
    out_specs = (
        P(None, "row", "col", None),
        P(None, "row", "col", None),
        P(None, "row", "col", None),
        P(None, "row", "col"),
    )
    return jax.shard_map(local, mesh=mesh, in_specs=in_specs, out_specs=out_specs, check_vma=False)
```

```python
import jax
import jax.numpy as jnp
from jax import lax
from jax.experimental import pallas as pl
from jax.experimental.pallas import tpu as pltpu
from jax.sharding import PartitionSpec as P

SUBCYCLES = 4
RELAX_RATE = 0.8
STEP_WEIGHT = 0.5
AIR_DRAG = 0.3
WATER_DRAG = 0.6
TOPMOST_WARMTH = -12.0
FREEZING = -1.8
DIFFUSION = 0.6
THERMAL_KAPPA = 0.1
OPEN_HEAT = 0.4
OPEN_WIND = 0.5

EDGE = 32
TILE = 4
MESH = pl.DeviceIdType.MESH


def lanes():
    return lax.broadcasted_iota(jnp.int32, (8, 128), 1)


def swap_groups(a, b, width, low):
    return (
        jnp.where(low, a, pltpu.roll(b, width, 1)),
        jnp.where(low, pltpu.roll(a, 128 - width, 1), b),
    )


def transpose4(parts):
    lane = lanes()
    low64 = lane < 64
    low32 = (lane % 64) < 32
    a, b, c, d = parts
    a, c = swap_groups(a, c, 64, low64)
    b, d = swap_groups(b, d, 64, low64)
    a, b = swap_groups(a, b, 32, low32)
    c, d = swap_groups(c, d, 32, low32)
    return [a, b, c, d]


def pick(parts, index):
    value = parts[0]
    for i in range(1, len(parts)):
        value = jnp.where(index == i, parts[i], value)
    return value


def solve_layers(warm_ref, out_ref, weight, surface, alive):
    layers = warm_ref.shape[0]
    thickness = weight * (1.0 / 0.9)
    inverse = 1.0 / thickness
    c = DIFFUSION * inverse * inverse
    diagonal = 1.0 + 2.0 * c
    ratios, partial = [], []
    for l in range(layers):
        supply = warm_ref[l, 0]
        if l == 0:
            supply = supply + c * TOPMOST_WARMTH
        if l == layers - 1:
            supply = supply + c * surface
        if l == 0:
            pivot = diagonal
        else:
            pivot = diagonal - c * ratios[-1]
            supply = supply + c * partial[-1]
        flip = 1.0 / pivot
        partial.append(supply * flip)
        ratios.append(c * flip)
    value = partial[-1]
    flux = THERMAL_KAPPA * (value - surface) * inverse
    out_ref[layers - 1, 0] = jnp.where(alive, value, 0.0)
    for l in range(layers - 2, -1, -1):
        value = partial[l] + ratios[l] * value
        out_ref[l, 0] = jnp.where(alive, value, 0.0)
    return flux


def kernel(
    rows,
    cols,
    skin_in, motion_in, tensor_in, weight_in, strength_in, warm_in, flags_in, source_in,
    motion_out, tensor_out, warm_out, ocean_out,
    B, TS, TSS, HF, F, K, KS, G, D, DS, send, recv,
    skin, motion, tensor, weight, strength, warm, flags, source, loaded,
):
    pairs = (
        (motion_in, motion), (tensor_in, tensor), (weight_in, weight), (strength_in, strength),
        (skin_in, skin), (source_in, source), (flags_in, flags), (warm_in, warm),
    )
    loads = [pltpu.make_async_copy(a, b, loaded.at[i]) for i, (a, b) in enumerate(pairs)]
    for load in loads:
        load.start()

    me_r = lax.axis_index("row")
    me_c = lax.axis_index("col")
    east = (me_r, lax.rem(me_c + 1, cols))
    west = (me_r, lax.rem(me_c + cols - 1, cols))
    north = (me_r + 1, me_c)
    south = (me_r - 1, me_c)
    has_north = me_r < rows - 1
    has_south = me_r > 0
    diagonal_north = ((me_r + 1, west[1]), (me_r + 1, east[1]))
    diagonal_south = ((me_r - 1, west[1]), (me_r - 1, east[1]))

    F[:, :, 8:16, :] = jnp.zeros((9, 4, 8, 128), jnp.float32)
    K[:, :, 8:16, :] = jnp.zeros((2, 4, 8, 128), jnp.float32)

    barrier = pltpu.get_barrier_semaphore()
    pl.semaphore_signal(barrier, inc=1, device_id=east, device_id_type=MESH)
    pl.semaphore_signal(barrier, inc=1, device_id=west, device_id_type=MESH)

    @pl.when(has_north)
    def _():
        for device in (north, *diagonal_north):
            pl.semaphore_signal(barrier, inc=1, device_id=device, device_id_type=MESH)

    @pl.when(has_south)
    def _():
        for device in (south, *diagonal_south):
            pl.semaphore_signal(barrier, inc=1, device_id=device, device_id_type=MESH)

    for load in loads[4:7]:
        load.wait()

    first = me_c * TILE
    block_index, block_covered = [], []
    out_rank = jnp.int32(0)
    out_first = jnp.int32(0)
    out_second = jnp.int32(0)
    for b in range(TILE):
        own = jnp.int32(-1)
        for j in range(TILE):
            own = jnp.where(source[0, j] == first + b, j, own)
        covered = flags[0, b] == 1
        moved = jnp.logical_and(covered, own < 0)
        block_index.append(jnp.where(own >= 0, own, TILE + jnp.minimum(out_rank, 1)))
        block_covered.append(covered)
        out_first = jnp.where(jnp.logical_and(moved, out_rank == 0), b, out_first)
        out_second = jnp.where(jnp.logical_and(moved, out_rank == 1), b, out_second)
        out_rank = out_rank + jnp.where(moved, 1, 0)
    slot_index = [
        jnp.where(source[0, j] >= first, jnp.minimum(source[0, j] - first, TILE - 1), TILE + min(j, 1))
        for j in range(TILE)
    ]

    for load in loads[:4]:
        load.wait()
    for f in range(2):
        B[0:4, f] = motion[f, 0].reshape(4, 8, 128)
    for f in range(3):
        B[0:4, 2 + f] = tensor[f, 0].reshape(4, 8, 128)
    B[0:4, 5] = weight[0].reshape(4, 8, 128)
    B[0:4, 6] = strength[0].reshape(4, 8, 128)

    surface = transpose4([skin[0, pl.ds(q, 8, stride=4), :] for q in range(4)])
    for b in range(4):
        TS[b] = surface[b]
    TSS[0] = pick(surface, out_first)
    TSS[1] = pick(surface, out_second)

    peers = 2 + 3 * jnp.minimum(me_r, 1) + 3 * jnp.minimum(rows - 1 - me_r, 1)
    pl.semaphore_wait(barrier, peers)

    def remote(k, src, dst, device):
        return pltpu.make_async_remote_copy(
            src_ref=src, dst_ref=dst, send_sem=send.at[k], recv_sem=recv.at[k],
            device_id=device, device_id_type=MESH,
        )

    slots_west = remote(0, B.at[0:2], B.at[4:6], west)
    slots_west.start()
    temps_east = remote(1, TSS, TS.at[4:6], east)
    temps_east.start()

    for q in range(4):
        at = pl.ds(q, 8, stride=4)
        F[7, q, 0:8] = AIR_DRAG * skin[3, at, :] + WATER_DRAG * skin[1, at, :]
        F[8, q, 0:8] = AIR_DRAG * skin[4, at, :] + WATER_DRAG * skin[2, at, :]

    slots_west.wait_recv()
    for p in range(7):
        held = [jnp.where(block_covered[b], B[block_index[b], p], 0.0) for b in range(4)]
        held = transpose4(held)
        for q in range(4):
            F[p, q, 0:8] = held[q]

    rows_north = remote(4, F.at[:, :, 6:8, :], F.at[:, :, 14:16, :], north)
    rows_south = remote(5, F.at[:, :, 0:2, :], F.at[:, :, 8:10, :], south)

    @pl.when(has_north)
    def _():
        rows_north.start()

    @pl.when(has_south)
    def _():
        rows_south.start()

    group = lanes() // 8
    for q in range(4):
        pack_e = jnp.zeros((8, 128), jnp.float32)
        pack_w = jnp.zeros((8, 128), jnp.float32)
        for p in range(9):
            turned = F[p, q, 0:8]
            if p:
                turned = pltpu.roll(turned, 8 * p, 1)
            pack_e = jnp.where(group == p, turned, pack_e)
            pack_w = jnp.where(group == (p + 15) % 16, turned, pack_w)
        KS[0, q] = pack_e
        KS[1, q] = pack_w

    corners_north = [
        remote(6 + 2 * i, KS.at[i, :, 6:8, :], K.at[i, :, 14:16, :], diagonal_north[i])
        for i in range(2)
    ]
    corners_south = [
        remote(7 + 2 * i, KS.at[i, :, 0:2, :], K.at[i, :, 8:10, :], diagonal_south[i])
        for i in range(2)
    ]

    @pl.when(has_north)
    def _():
        for corner in corners_north:
            corner.start()

    @pl.when(has_south)
    def _():
        for corner in corners_south:
            corner.start()

    strip_west = remote(2, KS.at[0], K.at[0, :, 0:8, :], west)
    strip_east = remote(3, KS.at[1], K.at[1, :, 0:8, :], east)
    strip_west.start()
    strip_east.start()

    temps_east.wait_recv()
    loads[7].wait()
    slot_row = lax.broadcasted_iota(jnp.int32, (4, 1024), 0)
    alive_rows = jnp.zeros((4, 1024), jnp.int32)
    for j in range(TILE):
        alive_rows = jnp.where(slot_row == j, source[0, j], alive_rows)
    alive = alive_rows >= 0
    slot_surface = jnp.stack([TS[slot_index[j]] for j in range(4)]).reshape(4, 1024)
    flux = solve_layers(warm, warm_out, weight[0], slot_surface, alive)
    HF[0:4] = flux.reshape(4, 8, 128)
    heat_west = remote(10, HF.at[0:2], HF.at[4:6], west)
    heat_west.start()

    strip_west.wait_recv()
    strip_east.wait_recv()

    @pl.when(has_south)
    def _():
        for copy in (rows_north, *corners_north):
            copy.wait_recv()

    @pl.when(has_north)
    def _():
        for copy in (rows_south, *corners_south):
            copy.wait_recv()

    wide = lax.broadcasted_iota(jnp.int32, (16, 128), 1) // 8
    for q in range(4):
        from_e = K[0, q]
        from_w = K[1, q]
        planes = []
        for p in range(9):
            side = jnp.where(wide == p, from_e, jnp.where(wide == (p + 15) % 16, from_w, 0.0))
            if p:
                side = pltpu.roll(side, 128 - 8 * p, 1)
            planes.append(jnp.concatenate([F[p, q], side], axis=1))
        for p in range(5):
            G[p, q] = planes[p]
        mass = planes[5]
        icy = mass > 0.0
        flip = jnp.where(icy, 1.0 / (mass + STEP_WEIGHT * WATER_DRAG), 0.0)
        G[5, q] = mass * flip
        G[6, q] = (0.5 * STEP_WEIGHT) * flip
        G[7, q] = planes[6]
        G[8, q] = STEP_WEIGHT * flip * planes[7]
        G[9, q] = STEP_WEIGHT * flip * planes[8]

    def across_x(x):
        return pltpu.roll(x, 255, 1) - pltpu.roll(x, 1, 1)

    def across_y(p, q):
        upper = G[p, q + 1] if q < 3 else pltpu.roll(G[p, 0], 15, 0)
        lower = G[p, q - 1] if q > 0 else pltpu.roll(G[p, 3], 1, 0)
        return upper - lower

    keep = 1.0 / (1.0 + RELAX_RATE)
    mix = RELAX_RATE / (1.0 + RELAX_RATE)

    def subcycle(step, carry):
        for q in range(4):
            ux = across_x(G[0, q])
            vx = across_x(G[1, q])
            uy = across_y(0, q)
            vy = across_y(1, q)
            power = G[7, q]
            divergence = 0.5 * (ux + vy)
            tension = 0.5 * (ux - vy)
            shearing = 0.25 * (uy + vx)
            square = (
                divergence * divergence
                + 0.25 * (tension * tension + 4.0 * shearing * shearing)
                + 0.25
            )
            viscosity = (0.5 * mix) * power * lax.rsqrt(square)
            common = 0.75 * viscosity * divergence - (0.25 * mix) * power
            half = 0.25 * viscosity
            G[2, q] = keep * G[2, q] + half * ux + common
            G[3, q] = keep * G[3, q] + half * vy + common
            G[4, q] = keep * G[4, q] + 0.5 * viscosity * shearing
        for q in range(4):
            force_e = across_x(G[2, q]) + across_y(4, q)
            force_n = across_x(G[4, q]) + across_y(3, q)
            share = G[6, q]
            stay = G[5, q]
            G[0, q] = stay * G[0, q] + share * force_e + G[8, q]
            G[1, q] = stay * G[1, q] + share * force_n + G[9, q]
        return carry

    lax.fori_loop(0, SUBCYCLES, subcycle, 0)

    for p in range(5):
        blocks = transpose4([G[p, q, 0:8, 0:128] for q in range(4)])
        for b in range(4):
            D[b, p] = blocks[b]
        DS[0, p] = pick(blocks, out_first)
        DS[1, p] = pick(blocks, out_second)
    back_east = remote(11, DS, D.at[4:6], east)
    back_east.start()

    heat_west.wait_recv()
    lane_block = lanes() // EDGE
    ice = jnp.zeros((8, 128), jnp.int32)
    for b in range(4):
        ice = jnp.where(lane_block == b, jnp.where(block_covered[b], 1, 0), ice)
    ice = ice == 1
    heat = transpose4([HF[block_index[b]] for b in range(4)])
    for q in range(4):
        at = pl.ds(q, 8, stride=4)
        ocean_out[0, at, :] = jnp.where(ice, heat[q], -OPEN_HEAT * (skin[0, at, :] - FREEZING))
        for f in range(2):
            ocean_out[1 + f, at, :] = jnp.where(
                ice,
                WATER_DRAG * (G[f, q, 0:8, 0:128] - skin[1 + f, at, :]),
                OPEN_WIND * skin[3 + f, at, :],
            )

    back_east.wait_recv()
    for p in range(5):
        value = jnp.stack([D[slot_index[j], p] for j in range(4)]).reshape(4, 1024)
        value = jnp.where(alive, value, 0.0)
        if p < 2:
            motion_out[p, 0] = value
        else:
            tensor_out[p - 2, 0] = value

    for copy in (slots_west, temps_east, strip_west, strip_east, heat_west, back_east):
        copy.wait_send()

    @pl.when(has_north)
    def _():
        for copy in (rows_north, *corners_north):
            copy.wait_send()

    @pl.when(has_south)
    def _():
        for copy in (rows_south, *corners_south):
            copy.wait_send()


def solution(mesh):
    rows, cols = mesh.shape["row"], mesh.shape["col"]

    def local(skin, motion, tensor, weight, strength, warm, filled, flags, source, adjacent):
        vmem = pl.BlockSpec(memory_space=pltpu.VMEM)
        hbm = pl.BlockSpec(memory_space=pltpu.HBM)
        f32 = jnp.float32
        arguments = (skin, motion, tensor, weight, strength, warm, flags, source)

        def body(*refs):
            kernel(rows, cols, *refs)

        out_shape = tuple(
            jax.ShapeDtypeStruct(s, f32)
            for s in (motion.shape, tensor.shape, warm.shape, (3,) + skin.shape[1:])
        )
        results = pl.pallas_call(
            body,
            out_shape=out_shape,
            in_specs=[hbm] * 8,
            out_specs=(vmem,) * 4,
            scratch_shapes=[
                pltpu.VMEM((6, 7, 8, 128), f32),
                pltpu.VMEM((6, 8, 128), f32),
                pltpu.VMEM((2, 8, 128), f32),
                pltpu.VMEM((6, 8, 128), f32),
                pltpu.VMEM((9, 4, 16, 128), f32),
                pltpu.VMEM((2, 4, 16, 128), f32),
                pltpu.VMEM((2, 4, 8, 128), f32),
                pltpu.VMEM((10, 4, 16, 256), f32),
                pltpu.VMEM((6, 5, 8, 128), f32),
                pltpu.VMEM((2, 5, 8, 128), f32),
                pltpu.SemaphoreType.DMA((12,)),
                pltpu.SemaphoreType.DMA((12,)),
                *(pltpu.VMEM(a.shape, f32) for a in (skin, motion, tensor, weight, strength, warm)),
                *(pltpu.SMEM(a.shape, jnp.int32) for a in (flags, source)),
                pltpu.SemaphoreType.DMA((8,)),
            ],
            compiler_params=pltpu.CompilerParams(
                collective_id=0, has_side_effects=True, vmem_limit_bytes=32 * 1024 * 1024
            ),
        )(*(pltpu.with_memory_space_constraint(a, pltpu.HBM) for a in arguments))
        return results

    in_specs = (
        P(None, "row", "col"),
        P(None, "row", "col", None),
        P(None, "row", "col", None),
        P("row", "col", None),
        P("row", "col", None),
        P(None, "row", "col"),
        P("row", "col"),
        P("row", "col"),
        P("row", "col"),
        P(None, "row", "col"),
    )
    out_specs = (
        P(None, "row", "col", None),
        P(None, "row", "col", None),
        P(None, "row", "col", None),
        P(None, "row", "col"),
    )
    return jax.shard_map(local, mesh=mesh, in_specs=in_specs, out_specs=out_specs, check_vma=False)
```

```python
import jax
import jax.numpy as jnp
from jax import lax
from jax.experimental import pallas as pl
from jax.experimental.pallas import tpu as pltpu
from jax.sharding import PartitionSpec as P

SUBCYCLES = 4
RELAX_RATE = 0.8
STEP_WEIGHT = 0.5
AIR_DRAG = 0.3
WATER_DRAG = 0.6
TOPMOST_WARMTH = -12.0
FREEZING = -1.8
DIFFUSION = 0.6
THERMAL_KAPPA = 0.1
OPEN_HEAT = 0.4
OPEN_WIND = 0.5

EDGE = 32
TILE = 4
MESH = pl.DeviceIdType.MESH


def lanes():
    return lax.broadcasted_iota(jnp.int32, (8, 128), 1)


def swap_groups(a, b, width, low):
    return (
        jnp.where(low, a, pltpu.roll(b, width, 1)),
        jnp.where(low, pltpu.roll(a, 128 - width, 1), b),
    )


def transpose4(parts):
    lane = lanes()
    low64 = lane < 64
    low32 = (lane % 64) < 32
    a, b, c, d = parts
    a, c = swap_groups(a, c, 64, low64)
    b, d = swap_groups(b, d, 64, low64)
    a, b = swap_groups(a, b, 32, low32)
    c, d = swap_groups(c, d, 32, low32)
    return [a, b, c, d]


def pick(parts, index):
    value = parts[0]
    for i in range(1, len(parts)):
        value = jnp.where(index == i, parts[i], value)
    return value


def solve_layers(warm_ref, out_ref, weight, surface, alive):
    layers = warm_ref.shape[0]
    thickness = weight * (1.0 / 0.9)
    inverse = 1.0 / thickness
    c = DIFFUSION * inverse * inverse
    diagonal = 1.0 + 2.0 * c
    ratios, partial = [], []
    for l in range(layers):
        supply = warm_ref[l, 0]
        if l == 0:
            supply = supply + c * TOPMOST_WARMTH
        if l == layers - 1:
            supply = supply + c * surface
        if l == 0:
            pivot = diagonal
        else:
            pivot = diagonal - c * ratios[-1]
            supply = supply + c * partial[-1]
        flip = 1.0 / pivot
        partial.append(supply * flip)
        ratios.append(c * flip)
    value = partial[-1]
    flux = THERMAL_KAPPA * (value - surface) * inverse
    out_ref[layers - 1, 0] = jnp.where(alive, value, 0.0)
    for l in range(layers - 2, -1, -1):
        value = partial[l] + ratios[l] * value
        out_ref[l, 0] = jnp.where(alive, value, 0.0)
    return flux


def kernel(
    rows,
    cols,
    skin_in, motion_in, tensor_in, weight_in, strength_in, warm_in, flags_in, source_in,
    motion_out, tensor_out, warm_out, ocean_out,
    B, TS, TSS, HF, F, R, RS, K, KS, G, D, DS, send, recv,
    skin, motion, tensor, weight, strength, warm, flags, source, loaded,
):
    pairs = (
        (motion_in, motion), (tensor_in, tensor), (weight_in, weight), (strength_in, strength),
        (skin_in, skin), (source_in, source), (flags_in, flags), (warm_in, warm),
    )
    loads = [pltpu.make_async_copy(a, b, loaded.at[i]) for i, (a, b) in enumerate(pairs)]
    for load in loads:
        load.start()

    me_r = lax.axis_index("row")
    me_c = lax.axis_index("col")
    east = (me_r, lax.rem(me_c + 1, cols))
    west = (me_r, lax.rem(me_c + cols - 1, cols))
    north = (me_r + 1, me_c)
    south = (me_r - 1, me_c)
    has_north = me_r < rows - 1
    has_south = me_r > 0
    diagonal_north = ((me_r + 1, west[1]), (me_r + 1, east[1]))
    diagonal_south = ((me_r - 1, west[1]), (me_r - 1, east[1]))

    R[...] = jnp.zeros((2, 9, 8, 128), jnp.float32)
    K[:, :, 8:16, :] = jnp.zeros((2, 4, 8, 128), jnp.float32)

    barrier = pltpu.get_barrier_semaphore()
    pl.semaphore_signal(barrier, inc=1, device_id=east, device_id_type=MESH)
    pl.semaphore_signal(barrier, inc=1, device_id=west, device_id_type=MESH)

    @pl.when(has_north)
    def _():
        for device in (north, *diagonal_north):
            pl.semaphore_signal(barrier, inc=1, device_id=device, device_id_type=MESH)

    @pl.when(has_south)
    def _():
        for device in (south, *diagonal_south):
            pl.semaphore_signal(barrier, inc=1, device_id=device, device_id_type=MESH)

    for load in loads[4:7]:
        load.wait()

    first = me_c * TILE
    block_index, block_covered = [], []
    out_rank = jnp.int32(0)
    out_first = jnp.int32(0)
    out_second = jnp.int32(0)
    for b in range(TILE):
        own = jnp.int32(-1)
        for j in range(TILE):
            own = jnp.where(source[0, j] == first + b, j, own)
        covered = flags[0, b] == 1
        moved = jnp.logical_and(covered, own < 0)
        block_index.append(jnp.where(own >= 0, own, TILE + jnp.minimum(out_rank, 1)))
        block_covered.append(covered)
        out_first = jnp.where(jnp.logical_and(moved, out_rank == 0), b, out_first)
        out_second = jnp.where(jnp.logical_and(moved, out_rank == 1), b, out_second)
        out_rank = out_rank + jnp.where(moved, 1, 0)
    slot_index = [
        jnp.where(source[0, j] >= first, jnp.minimum(source[0, j] - first, TILE - 1), TILE + min(j, 1))
        for j in range(TILE)
    ]

    for load in loads[:4]:
        load.wait()
    for f in range(2):
        B[0:4, f] = motion[f, 0].reshape(4, 8, 128)
    for f in range(3):
        B[0:4, 2 + f] = tensor[f, 0].reshape(4, 8, 128)
    B[0:4, 5] = weight[0].reshape(4, 8, 128)
    B[0:4, 6] = strength[0].reshape(4, 8, 128)

    surface = transpose4([skin[0, pl.ds(q, 8, stride=4), :] for q in range(4)])
    for b in range(4):
        TS[b] = surface[b]
    TSS[0] = pick(surface, out_first)
    TSS[1] = pick(surface, out_second)

    peers = 2 + 3 * jnp.minimum(me_r, 1) + 3 * jnp.minimum(rows - 1 - me_r, 1)
    pl.semaphore_wait(barrier, peers)

    def remote(k, src, dst, device):
        return pltpu.make_async_remote_copy(
            src_ref=src, dst_ref=dst, send_sem=send.at[k], recv_sem=recv.at[k],
            device_id=device, device_id_type=MESH,
        )

    slots_west = remote(0, B.at[0:2], B.at[4:6], west)
    slots_west.start()
    temps_east = remote(1, TSS, TS.at[4:6], east)
    temps_east.start()

    for q in range(4):
        at = pl.ds(q, 8, stride=4)
        F[7, q, 0:8] = AIR_DRAG * skin[3, at, :] + WATER_DRAG * skin[1, at, :]
        F[8, q, 0:8] = AIR_DRAG * skin[4, at, :] + WATER_DRAG * skin[2, at, :]

    pair = lax.broadcasted_iota(jnp.int32, (8, 128), 0) // 2

    def pack_rows(low, high):
        for p in range(low, high):
            first_rows = F[p, 0]
            last_rows = F[p, 0]
            for q in range(1, 4):
                turned = pltpu.roll(F[p, q], 2 * q, 0)
                first_rows = jnp.where(pair == q, turned, first_rows)
                last_rows = jnp.where(pair == q - 1, turned, last_rows)
            RS[0, p] = first_rows
            RS[1, p] = last_rows

    pack_rows(7, 9)
    force_north = remote(12, RS.at[1, 7:9], R.at[1, 7:9], north)
    force_south = remote(13, RS.at[0, 7:9], R.at[0, 7:9], south)

    @pl.when(has_north)
    def _():
        force_north.start()

    @pl.when(has_south)
    def _():
        force_south.start()

    slots_west.wait_recv()
    for p in range(7):
        held = [jnp.where(block_covered[b], B[block_index[b], p], 0.0) for b in range(4)]
        held = transpose4(held)
        for q in range(4):
            F[p, q, 0:8] = held[q]
    pack_rows(0, 7)
    rows_north = remote(4, RS.at[1, 0:7], R.at[1, 0:7], north)
    rows_south = remote(5, RS.at[0, 0:7], R.at[0, 0:7], south)

    @pl.when(has_north)
    def _():
        rows_north.start()

    @pl.when(has_south)
    def _():
        rows_south.start()

    group = lanes() // 8
    for q in range(4):
        pack_e = jnp.zeros((8, 128), jnp.float32)
        pack_w = jnp.zeros((8, 128), jnp.float32)
        for p in range(9):
            turned = F[p, q, 0:8]
            if p:
                turned = pltpu.roll(turned, 8 * p, 1)
            pack_e = jnp.where(group == p, turned, pack_e)
            pack_w = jnp.where(group == (p + 15) % 16, turned, pack_w)
        KS[0, q] = pack_e
        KS[1, q] = pack_w

    corners_north = [
        remote(6 + 2 * i, KS.at[i, :, 6:8, :], K.at[i, :, 14:16, :], diagonal_north[i])
        for i in range(2)
    ]
    corners_south = [
        remote(7 + 2 * i, KS.at[i, :, 0:2, :], K.at[i, :, 8:10, :], diagonal_south[i])
        for i in range(2)
    ]

    @pl.when(has_north)
    def _():
        for corner in corners_north:
            corner.start()

    @pl.when(has_south)
    def _():
        for corner in corners_south:
            corner.start()

    strip_west = remote(2, KS.at[0], K.at[0, :, 0:8, :], west)
    strip_east = remote(3, KS.at[1], K.at[1, :, 0:8, :], east)
    strip_west.start()
    strip_east.start()

    temps_east.wait_recv()
    loads[7].wait()
    slot_row = lax.broadcasted_iota(jnp.int32, (4, 1024), 0)
    alive_rows = jnp.zeros((4, 1024), jnp.int32)
    for j in range(TILE):
        alive_rows = jnp.where(slot_row == j, source[0, j], alive_rows)
    alive = alive_rows >= 0
    slot_surface = jnp.stack([TS[slot_index[j]] for j in range(4)]).reshape(4, 1024)
    flux = solve_layers(warm, warm_out, weight[0], slot_surface, alive)
    HF[0:4] = flux.reshape(4, 8, 128)
    heat_west = remote(10, HF.at[0:2], HF.at[4:6], west)
    heat_west.start()

    strip_west.wait_recv()
    strip_east.wait_recv()

    @pl.when(has_south)
    def _():
        for copy in (rows_north, force_north, *corners_north):
            copy.wait_recv()

    @pl.when(has_north)
    def _():
        for copy in (rows_south, force_south, *corners_south):
            copy.wait_recv()

    wide = lax.broadcasted_iota(jnp.int32, (16, 128), 1) // 8
    for q in range(4):
        from_e = K[0, q]
        from_w = K[1, q]
        planes = []
        for p in range(9):
            side = jnp.where(wide == p, from_e, jnp.where(wide == (p + 15) % 16, from_w, 0.0))
            if p:
                side = pltpu.roll(side, 128 - 8 * p, 1)
            beyond = jnp.where(pair == q, R[0, p], jnp.where(pair == (q + 3) % 4, R[1, p], 0.0))
            if q:
                beyond = pltpu.roll(beyond, 8 - 2 * q, 0)
            center = jnp.concatenate([F[p, q], beyond], axis=0)
            planes.append(jnp.concatenate([center, side], axis=1))
        for p in range(5):
            G[p, q] = planes[p]
        mass = planes[5]
        icy = mass > 0.0
        flip = jnp.where(icy, 1.0 / (mass + STEP_WEIGHT * WATER_DRAG), 0.0)
        G[5, q] = mass * flip
        G[6, q] = (0.5 * STEP_WEIGHT) * flip
        G[7, q] = planes[6]
        G[8, q] = STEP_WEIGHT * flip * planes[7]
        G[9, q] = STEP_WEIGHT * flip * planes[8]

    def across_x(x):
        return pltpu.roll(x, 255, 1) - pltpu.roll(x, 1, 1)

    def across_y(p, q):
        upper = G[p, q + 1] if q < 3 else pltpu.roll(G[p, 0], 15, 0)
        lower = G[p, q - 1] if q > 0 else pltpu.roll(G[p, 3], 1, 0)
        return upper - lower

    keep = 1.0 / (1.0 + RELAX_RATE)
    mix = RELAX_RATE / (1.0 + RELAX_RATE)

    def subcycle(step, carry):
        for q in range(4):
            ux = across_x(G[0, q])
            vx = across_x(G[1, q])
            uy = across_y(0, q)
            vy = across_y(1, q)
            power = G[7, q]
            divergence = 0.5 * (ux + vy)
            tension = 0.5 * (ux - vy)
            shearing = 0.25 * (uy + vx)
            square = (
                divergence * divergence
                + 0.25 * (tension * tension + 4.0 * shearing * shearing)
                + 0.25
            )
            viscosity = (0.5 * mix) * power * lax.rsqrt(square)
            common = 0.75 * viscosity * divergence - (0.25 * mix) * power
            half = 0.25 * viscosity
            G[2, q] = keep * G[2, q] + half * ux + common
            G[3, q] = keep * G[3, q] + half * vy + common
            G[4, q] = keep * G[4, q] + 0.5 * viscosity * shearing
        for q in range(4):
            force_e = across_x(G[2, q]) + across_y(4, q)
            force_n = across_x(G[4, q]) + across_y(3, q)
            share = G[6, q]
            stay = G[5, q]
            G[0, q] = stay * G[0, q] + share * force_e + G[8, q]
            G[1, q] = stay * G[1, q] + share * force_n + G[9, q]
        return carry

    lax.fori_loop(0, SUBCYCLES, subcycle, 0)

    for p in range(5):
        blocks = transpose4([G[p, q, 0:8, 0:128] for q in range(4)])
        for b in range(4):
            D[b, p] = blocks[b]
        DS[0, p] = pick(blocks, out_first)
        DS[1, p] = pick(blocks, out_second)
    back_east = remote(11, DS, D.at[4:6], east)
    back_east.start()

    heat_west.wait_recv()
    lane_block = lanes() // EDGE
    ice = jnp.zeros((8, 128), jnp.int32)
    for b in range(4):
        ice = jnp.where(lane_block == b, jnp.where(block_covered[b], 1, 0), ice)
    ice = ice == 1
    heat = transpose4([HF[block_index[b]] for b in range(4)])
    for q in range(4):
        at = pl.ds(q, 8, stride=4)
        ocean_out[0, at, :] = jnp.where(ice, heat[q], -OPEN_HEAT * (skin[0, at, :] - FREEZING))
        for f in range(2):
            ocean_out[1 + f, at, :] = jnp.where(
                ice,
                WATER_DRAG * (G[f, q, 0:8, 0:128] - skin[1 + f, at, :]),
                OPEN_WIND * skin[3 + f, at, :],
            )

    back_east.wait_recv()
    for p in range(5):
        value = jnp.stack([D[slot_index[j], p] for j in range(4)]).reshape(4, 1024)
        value = jnp.where(alive, value, 0.0)
        if p < 2:
            motion_out[p, 0] = value
        else:
            tensor_out[p - 2, 0] = value

    for copy in (slots_west, temps_east, strip_west, strip_east, heat_west, back_east):
        copy.wait_send()

    @pl.when(has_north)
    def _():
        for copy in (rows_north, force_north, *corners_north):
            copy.wait_send()

    @pl.when(has_south)
    def _():
        for copy in (rows_south, force_south, *corners_south):
            copy.wait_send()


def solution(mesh):
    rows, cols = mesh.shape["row"], mesh.shape["col"]

    def local(skin, motion, tensor, weight, strength, warm, filled, flags, source, adjacent):
        vmem = pl.BlockSpec(memory_space=pltpu.VMEM)
        hbm = pl.BlockSpec(memory_space=pltpu.HBM)
        f32 = jnp.float32
        arguments = (skin, motion, tensor, weight, strength, warm, flags, source)

        def body(*refs):
            kernel(rows, cols, *refs)

        out_shape = tuple(
            jax.ShapeDtypeStruct(s, f32)
            for s in (motion.shape, tensor.shape, warm.shape, (3,) + skin.shape[1:])
        )
        results = pl.pallas_call(
            body,
            out_shape=out_shape,
            in_specs=[hbm] * 8,
            out_specs=(vmem,) * 4,
            scratch_shapes=[
                pltpu.VMEM((6, 7, 8, 128), f32),
                pltpu.VMEM((6, 8, 128), f32),
                pltpu.VMEM((2, 8, 128), f32),
                pltpu.VMEM((6, 8, 128), f32),
                pltpu.VMEM((9, 4, 8, 128), f32),
                pltpu.VMEM((2, 9, 8, 128), f32),
                pltpu.VMEM((2, 9, 8, 128), f32),
                pltpu.VMEM((2, 4, 16, 128), f32),
                pltpu.VMEM((2, 4, 8, 128), f32),
                pltpu.VMEM((10, 4, 16, 256), f32),
                pltpu.VMEM((6, 5, 8, 128), f32),
                pltpu.VMEM((2, 5, 8, 128), f32),
                pltpu.SemaphoreType.DMA((14,)),
                pltpu.SemaphoreType.DMA((14,)),
                *(pltpu.VMEM(a.shape, f32) for a in (skin, motion, tensor, weight, strength, warm)),
                *(pltpu.SMEM(a.shape, jnp.int32) for a in (flags, source)),
                pltpu.SemaphoreType.DMA((8,)),
            ],
            compiler_params=pltpu.CompilerParams(
                collective_id=0, has_side_effects=True, vmem_limit_bytes=32 * 1024 * 1024
            ),
        )(*(pltpu.with_memory_space_constraint(a, pltpu.HBM) for a in arguments))
        return results

    in_specs = (
        P(None, "row", "col"),
        P(None, "row", "col", None),
        P(None, "row", "col", None),
        P("row", "col", None),
        P("row", "col", None),
        P(None, "row", "col"),
        P("row", "col"),
        P("row", "col"),
        P("row", "col"),
        P(None, "row", "col"),
    )
    out_specs = (
        P(None, "row", "col", None),
        P(None, "row", "col", None),
        P(None, "row", "col", None),
        P(None, "row", "col"),
    )
    return jax.shard_map(local, mesh=mesh, in_specs=in_specs, out_specs=out_specs, check_vma=False)
```
